32 devices in a mesh: seq: 8 (over y, x, core), head: 4 (over z).
Axes of the slice: x: 2, y: 2, z: 4, core: 2. Of those that a mesh axis runs over, the one named last changes fastest.
Arguments:
- inputs: bfloat16 [4096, 4096], P('seq'), may hold values from -6 to 6
- q_weight: bfloat16 [4096, 2048], P(None, 'head'), may hold values from -0.09375 to 0.09375
- kv_weight: bfloat16 [4096, 2, 512], P(None, None, 'head'), may hold values from -0.09375 to 0.09375
- norm_gain: float32 [2048], P('head'), may hold values from 0.1 to 1.9
- out_grad: bfloat16 [4096, 2048], P('seq', 'head'), may hold values from -6 to 6
Outputs:
- input_grad: bfloat16 [4096, 4096], P('seq', 'head')
- q_weight_grad: float32 [4096, 2048], P('seq', 'head')
- kv_weight_grad: float32 [4096, 2, 512], P('seq', None, 'head')
The draws below stay inside these ranges and needn't reach their ends.
All inputs are finite; a program needn't handle non-finite values.
Results may differ from the reference program's by a relative error of at most 0.022.
Values may be sent and summed in bfloat16 or wider, within the bound.
No kernel may reach another device: no remote copies, remote signals or barrier semaphores. Data moves between devices by JAX's collectives and lax.ppermute only.
A program may use at most 128 MiB of HBM per device.

```python
import jax
import jax.numpy as jnp
from jax import lax

D = 4096
HD = 128
HEADS_DEV = 4
KV_DEV = 1
TOK_DEV = 512
KV_HEADS = 4
HEADS = 16
TOKENS = 4096
N_HEAD = 4


def raised(array, key, source, target, shards_of, factor):
    owner, partner = [(jnp.arange(array.shape[position]) // (array.shape[position] // shards_of)).reshape([-1 if axis == position else 1 for axis in range(array.ndim)]) for position in (source, target)]
    chosen = jax.random.permutation(key, shards_of)[partner]
    strong = (owner == chosen) | (owner == (partner + shards_of // 2) % shards_of)
    return jnp.where(strong, factor * array, array)


def shard_levels(rng, extent, shards, least, largest):
    def one(axis_at, blocks):
        heights = jax.random.uniform(jax.random.fold_in(jax.random.fold_in(rng, 6), axis_at), (blocks,), jnp.float32, least / len(shards), largest / len(shards))
        return jnp.repeat(jnp.exp(heights), extent[axis_at] // blocks).reshape((-1,) + (1,) * (len(extent) - axis_at - 1))

    gain = one(*shards[0])
    for cut in shards[1:]:
        gain = gain * one(*cut)
    return gain


def normal_values(key, shape, deviation, limit, cuts=(), held_as=jnp.bfloat16):
    array = jax.random.normal(key, shape, jnp.float32) * deviation
    if len(cuts) > 0:
        array = shard_levels(key, shape, cuts, -0.22, 0.18) * array
    return jnp.clip(array, min=-limit, max=limit).astype(held_as)


def noise_with(own_key, dims, scale, most, split, heavy, kind=jnp.bfloat16):
    array = scale * jax.random.normal(own_key, dims, jnp.float32)
    if split:
        array = array * shard_levels(own_key, dims, split, -0.22, 0.18)
    return jnp.clip(raised(array, jax.random.fold_in(own_key, 3), *heavy), -most, most).astype(kind)


def setup_inputs(seed: int = 0) -> dict:
    splits = jax.random.split(jax.random.key(seed), 6)
    return {
        "inputs": noise_with(splits[0], (TOKENS, D), 1.0, 6.0, ((0, 8),), (0, 1, 8, 2.0)),
        "q_weight": normal_values(splits[1], (D, HEADS * HD), D ** -0.5, 0.09375, ((1, 4),)),
        "kv_weight": normal_values(splits[2], (D, 2, KV_HEADS * HD), D ** -0.5, 0.09375, ((2, 4),)),
        "norm_gain": jnp.clip(1.0 + 0.18 * jax.random.normal(splits[3], (HEADS * HD,), jnp.float32), 0.1, 1.9),
        "out_grad": normal_values(splits[4], (TOKENS, HEADS * HD), 1.0, 6.0, ((0, 8), (1, 4))),
    }


exact_prec = lax.Precision.HIGHEST
EPSILON = 1e-05

def causal_mask(length):
    row_ids = lax.broadcasted_iota(jnp.int32, (length, length), 0)
    column_ids = lax.broadcasted_iota(jnp.int32, (length, length), 1)
    return (column_ids <= row_ids).astype(jnp.float32)

def reference(inputs, q_weight, kv_weight, norm_gain, out_grad):
    kv_total = KV_DEV * N_HEAD
    kv_width = kv_total * HD
    blocks = TOKENS // TOK_DEV
    q_proj = jnp.dot(inputs, q_weight, preferred_element_type=jnp.float32).astype(jnp.bfloat16)
    kv_flat = kv_weight.reshape(D, 2 * kv_width)
    kv_proj = jnp.dot(inputs, kv_flat, preferred_element_type=jnp.float32).astype(jnp.bfloat16)
    q_all = q_proj.astype(jnp.float32).reshape(blocks, TOK_DEV, kv_total, HEADS_DEV, HD)
    k_all = kv_proj[:, :kv_width].astype(jnp.float32).reshape(blocks, TOK_DEV, kv_total, HD)
    v_all = kv_proj[:, kv_width:].astype(jnp.float32).reshape(blocks, TOK_DEV, kv_total, HD)
    grad_in = out_grad.astype(jnp.float32).reshape(blocks, TOK_DEV, kv_total, HEADS_DEV, HD)
    gain_heads = norm_gain.reshape(kv_total, HEADS_DEV, HD)
    tri_mask = causal_mask(TOK_DEV)

    def forward_block(earlier, block):
        queries, key_rows, val_rows, upstream = block
        scores = jnp.einsum('tghi,sgi->ghts', queries, key_rows, precision=exact_prec) * tri_mask
        attended = jnp.einsum('ghts,sgj->tghj', scores, val_rows, precision=exact_prec)
        attended = attended + jnp.einsum('tghi,gij->tghj', queries, earlier, precision=exact_prec)
        inv_rms = lax.rsqrt(lax.optimization_barrier(jnp.mean(attended * attended, axis=-1, keepdims=True)) + EPSILON)
        scaled_grad = gain_heads * upstream
        along = lax.optimization_barrier(jnp.mean(scaled_grad * attended, axis=-1, keepdims=True))
        attn_grad = inv_rms * (scaled_grad - attended * (inv_rms * inv_rms) * along)
        grad_scores = jnp.einsum('tghj,sgj->ghts', attn_grad, val_rows, precision=exact_prec) * tri_mask
        query_grad = jnp.einsum('ghts,sgi->tghi', grad_scores, key_rows, precision=exact_prec)
        query_grad = query_grad + jnp.einsum('tghj,gij->tghi', attn_grad, earlier, precision=exact_prec)
        updated = earlier + jnp.einsum('sgi,sgj->gij', key_rows, val_rows, precision=exact_prec)
        return (updated, (attn_grad, query_grad))
    start_state = jnp.zeros((kv_total, HD, HD), jnp.float32)
    final_state, outcome = lax.scan(forward_block, start_state, (q_all, k_all, v_all, grad_in))
    attn_grads, query_grads = outcome

    def backward_block(later, block):
        queries, key_rows, val_rows, attn_grad = block
        scores = jnp.einsum('tghi,sgi->ghts', queries, key_rows, precision=exact_prec) * tri_mask
        grad_scores = jnp.einsum('tghj,sgj->ghts', attn_grad, val_rows, precision=exact_prec) * tri_mask
        key_grad = jnp.einsum('ghts,tghi->sgi', grad_scores, queries, precision=exact_prec)
        key_grad = key_grad + jnp.einsum('sgj,gij->sgi', val_rows, later, precision=exact_prec)
        val_grad = jnp.einsum('ghts,tghj->sgj', scores, attn_grad, precision=exact_prec)
        val_grad = val_grad + jnp.einsum('sgi,gij->sgj', key_rows, later, precision=exact_prec)
        updated = later + jnp.einsum('tghi,tghj->gij', queries, attn_grad, precision=exact_prec)
        return (updated, (key_grad, val_grad))
    final_grad, outcome = lax.scan(backward_block, start_state, (q_all, k_all, v_all, attn_grads), reverse=True)
    key_grads, val_grads = outcome
    q_grads = query_grads.reshape(TOKENS, kv_total * HEADS_DEV * HD).astype(jnp.bfloat16)
    k_grads = key_grads.reshape(TOKENS, kv_width).astype(jnp.bfloat16)
    v_grads = val_grads.reshape(TOKENS, kv_width).astype(jnp.bfloat16)
    q_span = HEADS_DEV * HD
    input_total = jnp.zeros((TOKENS, D), jnp.float32)
    for group in range(kv_total):
        q_low = group * q_span
        kv_low = group * HD
        joined_grad = jnp.concatenate([q_grads[:, q_low:q_low + q_span], k_grads[:, kv_low:kv_low + HD], v_grads[:, kv_low:kv_low + HD]], axis=1)
        joined_weight = jnp.concatenate([q_weight[:, q_low:q_low + q_span], kv_weight[:, 0, kv_low:kv_low + HD], kv_weight[:, 1, kv_low:kv_low + HD]], axis=1)
        partial_value = jnp.dot(joined_grad, joined_weight.T, preferred_element_type=jnp.float32)
        input_total = input_total + partial_value.astype(jnp.bfloat16).astype(jnp.float32)
    input_grad = input_total.astype(jnp.bfloat16)
    inputs_t = inputs.T
    q_weight_grad = jnp.dot(inputs_t, q_grads, preferred_element_type=jnp.float32)
    k_weight_grad = jnp.dot(inputs_t, k_grads, preferred_element_type=jnp.float32)
    v_weight_grad = jnp.dot(inputs_t, v_grads, preferred_element_type=jnp.float32)
    kv_weight_grad = jnp.stack([k_weight_grad, v_weight_grad], axis=1)
    return (input_grad, q_weight_grad, kv_weight_grad)
```

```python
import functools

import jax
import jax.numpy as jnp
from jax import lax
from jax.experimental import pallas as pl
from jax.experimental.pallas import tpu as pltpu
from jax.sharding import PartitionSpec as P

HD = 128
EPSILON = 1e-05
F32 = jnp.float32
BF16 = jnp.bfloat16
VMEM_LIMIT = 40 * 1024 * 1024


def mm(a, b):
    return jnp.dot(a, b, preferred_element_type=F32)


def mm_nt(a, b):
    return lax.dot_general(a, b, (((1,), (1,)), ((), ())), preferred_element_type=F32)


def mm_tn(a, b):
    return lax.dot_general(a, b, (((0,), (0,)), ((), ())), preferred_element_type=F32)


def params():
    return pltpu.CompilerParams(vmem_limit_bytes=VMEM_LIMIT)


def cost(flops, nbytes):
    return pl.CostEstimate(flops=int(flops), bytes_accessed=int(nbytes), transcendentals=0)


VSPEC = pl.BlockSpec(memory_space=pltpu.VMEM)
SSPEC = pl.BlockSpec(memory_space=pltpu.SMEM)


def kv_kernel(x_ref, w_ref, kv_ref, state_ref, wkv_ref, acc_ref):
    step = pl.program_id(0)
    steps = pl.num_programs(0)
    rows = 2 * HD
    row = lax.broadcasted_iota(jnp.int32, (rows, rows), 0)
    col = lax.broadcasted_iota(jnp.int32, (rows, rows), 1)
    target = jnp.where(row < HD, 2 * row, 2 * (row - HD) + 1)
    perm = jnp.where(col == target, 1.0, 0.0).astype(BF16)
    for i in range(w_ref.shape[0] // rows):
        both = mm(perm, w_ref[i * rows : (i + 1) * rows, :]).astype(BF16)
        wkv_ref[i * HD : (i + 1) * HD, :HD] = both[:HD]
        wkv_ref[i * HD : (i + 1) * HD, HD:] = both[HD:]
    part = mm(x_ref[...], wkv_ref[...])

    @pl.when(step == 0)
    def _():
        acc_ref[...] = part

    @pl.when(step > 0)
    def _():
        acc_ref[...] += part

    @pl.when(step == steps - 1)
    def _():
        kv = acc_ref[...].astype(BF16)
        kv_ref[...] = kv
        state_ref[...] = mm_tn(kv[:, :HD], kv[:, HD:]).astype(BF16)


def kv_project(x, kv_flat):
    tok, d = x.shape
    steps = 4
    blk = d // steps
    return pl.pallas_call(
        kv_kernel,
        grid=(steps,),
        in_specs=[
            pl.BlockSpec((tok, blk), lambda i: (0, i)),
            pl.BlockSpec((2 * blk, HD), lambda i: (i, 0)),
        ],
        out_specs=[
            pl.BlockSpec((tok, 2 * HD), lambda i: (0, 0)),
            pl.BlockSpec((HD, HD), lambda i: (0, 0)),
            pl.BlockSpec((blk, 2 * HD), lambda i: (i, 0)),
        ],
        out_shape=[
            jax.ShapeDtypeStruct((tok, 2 * HD), BF16),
            jax.ShapeDtypeStruct((HD, HD), BF16),
            jax.ShapeDtypeStruct((d, 2 * HD), BF16),
        ],
        scratch_shapes=[pltpu.VMEM((tok, 2 * HD), F32)],
        compiler_params=params(),
        cost_estimate=cost(4 * tok * d * HD, 2 * (tok * d + 4 * d * HD)),
        name="kv_project",
    )(x, kv_flat)


def halves(tok):
    blk = min(256, tok)
    return [(lo, lo + blk) for lo in range(0, tok, blk)]


def masked(scores, row_first):
    rows, cols = scores.shape
    row = lax.broadcasted_iota(jnp.int32, (rows, cols), 0) + row_first
    col = lax.broadcasted_iota(jnp.int32, (rows, cols), 1)
    return jnp.where(col <= row, scores, 0.0)


def q_kernel(x_ref, w_ref, kv_ref, q_ref, o_ref, acc_ref):
    step = pl.program_id(0)
    steps = pl.num_programs(0)
    part = mm(x_ref[...], w_ref[...])

    @pl.when(step == 0)
    def _():
        acc_ref[...] = part

    @pl.when((step > 0) & (step < steps - 1))
    def _():
        acc_ref[...] += part

    @pl.when(step == steps - 1)
    def _():
        q = (acc_ref[...] + part).astype(BF16)
        q_ref[...] = q
        k, v = kv_ref[:, :HD], kv_ref[:, HD:]
        for lo, hi in halves(q.shape[0]):
            for h in range(q.shape[1] // HD):
                s = masked(mm_nt(q[lo:hi, h * HD : (h + 1) * HD], k[:hi]), lo)
                o_ref[lo:hi, h * HD : (h + 1) * HD] = mm(s.astype(BF16), v[:hi])


def q_project(x, q_weight, kv):
    tok, d = x.shape
    cols = q_weight.shape[1]
    steps = 4
    blk = d // steps
    return pl.pallas_call(
        q_kernel,
        grid=(steps,),
        in_specs=[
            pl.BlockSpec((tok, blk), lambda i: (0, i)),
            pl.BlockSpec((blk, cols), lambda i: (i, 0)),
            pl.BlockSpec((tok, 2 * HD), lambda i: (0, 0)),
        ],
        out_specs=[
            pl.BlockSpec((tok, cols), lambda i: (0, 0)),
            pl.BlockSpec((tok, cols), lambda i: (0, 0)),
        ],
        out_shape=[
            jax.ShapeDtypeStruct((tok, cols), BF16),
            jax.ShapeDtypeStruct((tok, cols), F32),
        ],
        scratch_shapes=[pltpu.VMEM((tok, cols), F32)],
        compiler_params=params(),
        cost_estimate=cost(2 * tok * d * cols, 2 * (tok * d + d * cols)),
        name="q_project",
    )(x, q_weight, kv)


def weighted(bits_ref, refs):
    total = None
    for i, ref in enumerate(refs):
        term = ref[...].astype(F32) * bits_ref[i].astype(F32)
        total = term if total is None else total + term
    return total


def grad_kernel(n, bits_ref, q_ref, o_ref, kv_ref, gain_ref, up_ref, *refs):
    states, (dq_ref, do_ref, own_ref) = refs[:n], refs[n:]
    prev = weighted(bits_ref, states).astype(BF16)
    k, v = kv_ref[:, :HD], kv_ref[:, HD:]
    own = None
    for lo, hi in halves(q_ref.shape[0]):
        for h in range(q_ref.shape[1] // HD):
            c = slice(h * HD, (h + 1) * HD)
            q = q_ref[lo:hi, c]
            o = o_ref[lo:hi, c] + mm(q, prev)
            inv = lax.rsqrt(jnp.mean(o * o, axis=-1, keepdims=True) + EPSILON)
            scaled = gain_ref[:, c] * up_ref[lo:hi, c].astype(F32)
            along = jnp.mean(scaled * o, axis=-1, keepdims=True)
            do = (inv * (scaled - o * ((inv * inv) * along))).astype(BF16)
            do_ref[lo:hi, c] = do
            s = masked(mm_nt(do, v[:hi]), lo).astype(BF16)
            dq_ref[lo:hi, c] = (mm(s, k[:hi]) + mm_nt(do, prev)).astype(BF16)
            part = mm_tn(q, do)
            own = part if own is None else own + part
    own_ref[...] = own.astype(BF16)


def grad_step(bits, q, o, kv, gain, upstream, states):
    tok, cols = q.shape
    n = len(states)
    return pl.pallas_call(
        functools.partial(grad_kernel, n),
        in_specs=[SSPEC] + [VSPEC] * (5 + n),
        out_specs=[VSPEC] * 3,
        out_shape=[
            jax.ShapeDtypeStruct((tok, cols), BF16),
            jax.ShapeDtypeStruct((tok, cols), BF16),
            jax.ShapeDtypeStruct((HD, HD), BF16),
        ],
        compiler_params=params(),
        cost_estimate=cost(8 * tok * tok * cols, 12 * tok * cols),
        name="grad_step",
    )(bits, q, o, kv, gain.reshape(1, cols), upstream, *states)


def inner_kernel(q_ref, do_ref, kv_ref, out_ref):
    k, v = kv_ref[:, :HD], kv_ref[:, HD:]
    tok = q_ref.shape[0]
    for lo, hi in halves(tok):
        col = lax.broadcasted_iota(jnp.int32, (hi - lo, tok - lo), 1)
        row = lax.broadcasted_iota(jnp.int32, (hi - lo, tok - lo), 0)
        dk = dv = None
        for h in range(q_ref.shape[1] // HD):
            c = slice(h * HD, (h + 1) * HD)
            q, do = q_ref[lo:, c], do_ref[lo:, c]
            s = jnp.where(col >= row, mm_nt(k[lo:hi], q), 0.0).astype(BF16)
            ds = jnp.where(col >= row, mm_nt(v[lo:hi], do), 0.0).astype(BF16)
            dk_h, dv_h = mm(ds, q), mm(s, do)
            dk = dk_h if dk is None else dk + dk_h
            dv = dv_h if dv is None else dv + dv_h
        out_ref[lo:hi, :HD] = dk
        out_ref[lo:hi, HD:] = dv


def inner_step(q, do, kv):
    tok, cols = q.shape
    return pl.pallas_call(
        inner_kernel,
        in_specs=[VSPEC] * 3,
        out_specs=VSPEC,
        out_shape=jax.ShapeDtypeStruct((tok, 2 * HD), F32),
        compiler_params=params(),
        cost_estimate=cost(8 * tok * tok * cols, 8 * tok * cols),
        name="inner_step",
    )(q, do, kv)


def outer_kernel(n, bits_ref, inner_ref, kv_ref, *refs):
    states, out_ref = refs[:n], refs[n]
    later = weighted(bits_ref, states).astype(BF16)
    k, v = kv_ref[:, :HD], kv_ref[:, HD:]
    out_ref[:, :HD] = (inner_ref[:, :HD] + mm_nt(v, later)).astype(BF16)
    out_ref[:, HD:] = (inner_ref[:, HD:] + mm(k, later)).astype(BF16)


def outer_step(bits, inner, kv, states):
    tok = kv.shape[0]
    n = len(states)
    return pl.pallas_call(
        functools.partial(outer_kernel, n),
        in_specs=[SSPEC] + [VSPEC] * (2 + n),
        out_specs=VSPEC,
        out_shape=jax.ShapeDtypeStruct((tok, 2 * HD), BF16),
        compiler_params=params(),
        cost_estimate=cost(4 * tok * HD * HD, 8 * tok * HD),
        name="outer_step",
    )(bits, inner, kv, *states)


def send_kernel(ids_ref, x_ref, g_ref, out_ref, gt_ref):
    @pl.when(pl.program_id(0) == 0)
    def _():
        gt_ref[...] = g_ref[...].T

    out_ref[0] = mm(gt_ref[...], x_ref[...]).astype(BF16)


def weight_send(ids, x, g, count):
    tok, d = x.shape
    cols = g.shape[1]
    blk = d // (2 * count)
    return pl.pallas_call(
        send_kernel,
        grid_spec=pltpu.PrefetchScalarGridSpec(
            num_scalar_prefetch=1,
            grid=(count,),
            in_specs=[
                pl.BlockSpec((tok, blk), lambda i, ids: (0, ids[i])),
                pl.BlockSpec((tok, cols), lambda i, ids: (0, 0)),
            ],
            out_specs=pl.BlockSpec((1, cols, blk), lambda i, ids: (i, 0, 0)),
            scratch_shapes=[pltpu.VMEM((cols, tok), BF16)],
        ),
        out_shape=jax.ShapeDtypeStruct((count, cols, blk), BF16),
        compiler_params=params(),
        cost_estimate=cost(2 * tok * cols * blk * count, 2 * count * blk * (tok + cols)),
        name="weight_send",
    )(ids, x, g)


def keep_kernel(half, ids_ref, x_ref, g_ref, got_ref, high_ref, low_ref, gt_ref):
    step = pl.program_id(0)

    @pl.when(step == 0)
    def _():
        gt_ref[...] = g_ref[...].T

    total = mm(gt_ref[...], x_ref[...]) + got_ref[0].astype(F32)

    @pl.when(step < half)
    def _():
        high_ref[0] = total.astype(BF16)

    @pl.when(step >= half)
    def _():
        low_ref[0] = total.astype(BF16)


def weight_keep(ids, x, g, got, count):
    tok, d = x.shape
    cols = g.shape[1]
    blk = d // (2 * count)
    half = count // 2
    where = lambda i: jnp.where(i < half, i + half, i - half)
    return pl.pallas_call(
        functools.partial(keep_kernel, half),
        grid_spec=pltpu.PrefetchScalarGridSpec(
            num_scalar_prefetch=1,
            grid=(count,),
            in_specs=[
                pl.BlockSpec((tok, blk), lambda i, ids: (0, ids[where(i)])),
                pl.BlockSpec((tok, cols), lambda i, ids: (0, 0)),
                pl.BlockSpec((1, cols, blk), lambda i, ids: (where(i), 0, 0)),
            ],
            out_specs=[
                pl.BlockSpec((1, cols, blk), lambda i, ids: (jnp.minimum(i, half - 1), 0, 0)),
                pl.BlockSpec((1, cols, blk), lambda i, ids: (jnp.maximum(i - half, 0), 0, 0)),
            ],
            scratch_shapes=[pltpu.VMEM((cols, tok), BF16)],
        ),
        out_shape=[jax.ShapeDtypeStruct((half, cols, blk), BF16)] * 2,
        compiler_params=params(),
        cost_estimate=cost(2 * tok * cols * blk * count, 2 * count * blk * (tok + 2 * cols)),
        name="weight_keep",
    )(ids, x, g, got)


def last_q_kernel(a_ref, b_ref, out_ref):
    out_ref[...] = (a_ref[0].astype(F32) + b_ref[0].astype(F32)).T


def last_kv_kernel(a_ref, b_ref, out_ref):
    total = a_ref[0].astype(F32) + b_ref[0].astype(F32)
    blk = total.shape[1]
    out_ref[pl.ds(0, blk, 2), :] = total[:HD].T
    out_ref[pl.ds(1, blk, 2), :] = total[HD:].T


def last_q(a, b):
    _, cols, blk = a.shape
    return pl.pallas_call(
        last_q_kernel,
        in_specs=[VSPEC] * 2,
        out_specs=VSPEC,
        out_shape=jax.ShapeDtypeStruct((blk, cols), F32),
        compiler_params=params(),
        cost_estimate=cost(blk * cols, 8 * blk * cols),
        name="last_q",
    )(a, b)


def last_kv(a, b):
    _, cols, blk = a.shape
    out = pl.pallas_call(
        last_kv_kernel,
        in_specs=[VSPEC] * 2,
        out_specs=VSPEC,
        out_shape=jax.ShapeDtypeStruct((2 * blk, HD), F32),
        compiler_params=params(),
        cost_estimate=cost(blk * cols, 8 * blk * cols),
        name="last_kv",
    )(a, b)
    return out.reshape(blk, 2, HD)


def flip(array, axis, bit):
    count = lax.axis_size(axis)
    return lax.ppermute(array, axis, [(i, i ^ (1 << bit)) for i in range(count)])


def doubling(state, axis, levels):
    received = []
    for bit in range(levels):
        got = flip(state, axis, bit)
        received.append(got)
        if bit < levels - 1:
            state = (state.astype(F32) + got.astype(F32)).astype(BF16)
    return received


def weight_grad(x, g, order, seq):
    count = lax.axis_size(seq)
    place = lax.axis_index(seq)
    half = count // 2
    relative = []
    for p in range(half):
        r = 0
        for at, bit in enumerate(order):
            r |= ((p >> (len(order) - 1 - at)) & 1) << bit
        relative.append(r)
    relative = jnp.array(relative, jnp.int32)
    sent = weight_send(place ^ (relative | 1), x, g, half)
    got = flip(sent, seq, 0)
    high, low = weight_keep(place ^ relative, x, g, got, half)
    for at, bit in enumerate(order):
        got = flip(high, seq, bit)
        if at == len(order) - 1:
            return low, got
        total = (low.astype(F32) + got.astype(F32)).astype(BF16)
        size = total.shape[0] // 2
        low, high = total[:size], total[size:]


def body(x, q_weight, kv_weight, norm_gain, out_grad):
    seq, head = "seq", "head"
    levels = (lax.axis_size(seq) - 1).bit_length()
    place = lax.axis_index(seq)
    bits = jnp.stack([(place >> i) & 1 for i in range(levels)]).astype(jnp.int32)
    d = x.shape[1]
    kv, state, wkv = kv_project(x, kv_weight.reshape(2 * d, HD))
    states = doubling(state, seq, levels)
    q, o = q_project(x, q_weight, kv)
    dq, do, own = grad_step(bits, q, o, kv, norm_gain, out_grad, states)
    laters = doubling(own, seq, levels)
    order = list(range(levels - 1, 0, -1))
    q_low, q_got = weight_grad(x, dq, order, seq)
    inner = inner_step(q, do, kv)
    dkv = outer_step(1 - bits, inner, kv, laters)
    kv_low, kv_got = weight_grad(x, dkv, order[::-1], seq)
    partial = jnp.dot(dq, q_weight.T, preferred_element_type=F32)
    partial = partial + jnp.dot(dkv, wkv.T, preferred_element_type=F32)
    input_grad = lax.psum_scatter(partial.astype(BF16), head, scatter_dimension=1, tiled=True)
    return input_grad, last_q(q_low, q_got), last_kv(kv_low, kv_got)


def solution(mesh):
    return jax.shard_map(
        body,
        mesh=mesh,
        in_specs=(
            P("seq", None),
            P(None, "head"),
            P(None, None, "head"),
            P("head"),
            P("seq", "head"),
        ),
        out_specs=(P("seq", "head"), P("seq", "head"), P("seq", None, "head")),
        check_vma=False,
    )
```

```python
import functools

import jax
import jax.numpy as jnp
from jax import lax
from jax.experimental import pallas as pl
from jax.experimental.pallas import tpu as pltpu
from jax.sharding import PartitionSpec as P

HD = 128
PARTS = 2
EPSILON = 1e-05
F32 = jnp.float32
BF16 = jnp.bfloat16
VMEM_LIMIT = 18 * 1024 * 1024
VMEM_MOST = 58 * 1024 * 1024


def mm(a, b):
    return jnp.dot(a, b, preferred_element_type=F32)


def mm_nt(a, b):
    return lax.dot_general(a, b, (((1,), (1,)), ((), ())), preferred_element_type=F32)


def mm_tn(a, b):
    return lax.dot_general(a, b, (((0,), (0,)), ((), ())), preferred_element_type=F32)


def params(limit):
    return pltpu.CompilerParams(vmem_limit_bytes=limit)


def cost(flops, nbytes):
    return pl.CostEstimate(
        flops=int(flops) // 64, bytes_accessed=int(nbytes) // 64, transcendentals=0
    )


def ordered(kernel, after, args, *, in_specs, lead=0, grid=None, out_specs, scratch=(), limit=VMEM_LIMIT, **kw):
    given = len(args) - lead
    extra = len(after)

    def run(*refs):
        kernel(*refs[: lead + given], *refs[lead + given + extra :])

    in_specs = list(in_specs) + [pl.BlockSpec(memory_space=pl.ANY)] * extra
    return pl.pallas_call(
        run,
        grid_spec=pltpu.PrefetchScalarGridSpec(
            num_scalar_prefetch=lead,
            grid=grid or (),
            in_specs=in_specs,
            out_specs=out_specs,
            scratch_shapes=scratch,
        ),
        compiler_params=params(limit),
        **kw,
    )(*args, *after)


ANY = pl.BlockSpec(memory_space=pl.ANY)
VSPEC = pl.BlockSpec(memory_space=pltpu.VMEM)
SSPEC = pl.BlockSpec(memory_space=pltpu.SMEM)


def parting(rows):
    half = rows // 2
    row = lax.broadcasted_iota(jnp.int32, (rows, rows), 0)
    col = lax.broadcasted_iota(jnp.int32, (rows, rows), 1)
    target = jnp.where(row < half, 2 * row, 2 * (row - half) + 1)
    return jnp.where(col == target, 1.0, 0.0).astype(BF16)


def kv_kernel(x_ref, w_ref, kv_ref, state_ref, wkv_ref, acc_ref):
    step = pl.program_id(0)
    steps = pl.num_programs(0)
    rows = 2 * HD
    perm = parting(rows)
    for i in range(w_ref.shape[0] // rows):
        both = mm(perm, w_ref[i * rows : (i + 1) * rows, :]).astype(BF16)
        wkv_ref[i * HD : (i + 1) * HD, :HD] = both[:HD]
        wkv_ref[i * HD : (i + 1) * HD, HD:] = both[HD:]
    part = mm(x_ref[...], wkv_ref[...])

    @pl.when(step == 0)
    def _():
        acc_ref[...] = part

    @pl.when(step > 0)
    def _():
        acc_ref[...] += part

    @pl.when(step == steps - 1)
    def _():
        kv = acc_ref[...].astype(BF16)
        kv_ref[...] = kv
        state_ref[...] = mm_tn(kv[:, :HD], kv[:, HD:]).astype(BF16)


def kv_project(x, kv_flat, after=()):
    tok, d = x.shape
    steps = 4
    blk = d // steps
    return ordered(
        kv_kernel,
        after,
        (x, kv_flat),
        grid=(steps,),
        in_specs=[
            pl.BlockSpec((tok, blk), lambda i: (0, i)),
            pl.BlockSpec((2 * blk, HD), lambda i: (i, 0)),
        ],
        out_specs=[
            pl.BlockSpec((tok, 2 * HD), lambda i: (0, 0)),
            pl.BlockSpec((HD, HD), lambda i: (0, 0)),
            pl.BlockSpec((blk, 2 * HD), lambda i: (i, 0)),
        ],
        out_shape=[
            jax.ShapeDtypeStruct((tok, 2 * HD), BF16),
            jax.ShapeDtypeStruct((HD, HD), BF16),
            jax.ShapeDtypeStruct((d, 2 * HD), BF16),
        ],
        scratch=[pltpu.VMEM((tok, 2 * HD), F32)],
        cost_estimate=cost(4 * tok * d * HD, 2 * (tok * d + 4 * d * HD)),
        name="kv_project",
    )


def halves(tok):
    blk = min(256, tok)
    return [(lo, lo + blk) for lo in range(0, tok, blk)]


def masked(scores, row_first):
    rows, cols = scores.shape
    row = lax.broadcasted_iota(jnp.int32, (rows, cols), 0) + row_first
    col = lax.broadcasted_iota(jnp.int32, (rows, cols), 1)
    return jnp.where(col <= row, scores, 0.0)


def q_kernel(x_ref, w_ref, q_ref, acc_ref):
    step = pl.program_id(0)
    steps = pl.num_programs(0)
    part = mm(x_ref[...], w_ref[...])

    @pl.when(step == 0)
    def _():
        acc_ref[...] = part

    @pl.when((step > 0) & (step < steps - 1))
    def _():
        acc_ref[...] += part

    @pl.when(step == steps - 1)
    def _():
        q_ref[...] = (acc_ref[...] + part).astype(BF16)


def q_project(x, q_weight, after=()):
    tok, d = x.shape
    cols = q_weight.shape[1]
    steps = 4
    blk = d // steps
    return ordered(
        q_kernel,
        after,
        (x, q_weight),
        grid=(steps,),
        in_specs=[
            pl.BlockSpec((tok, blk), lambda i: (0, i)),
            pl.BlockSpec((blk, cols), lambda i: (i, 0)),
        ],
        out_specs=pl.BlockSpec((tok, cols), lambda i: (0, 0)),
        out_shape=jax.ShapeDtypeStruct((tok, cols), BF16),
        scratch=[pltpu.VMEM((tok, cols), F32)],
        cost_estimate=cost(2 * tok * d * cols, 2 * (tok * d + d * cols)),
        name="q_project",
    )


def intra_kernel(q_ref, kv_ref, o_ref):
    k, v = kv_ref[:, :HD], kv_ref[:, HD:]
    for lo, hi in halves(q_ref.shape[0]):
        for h in range(q_ref.shape[1] // HD):
            c = slice(h * HD, (h + 1) * HD)
            s = masked(mm_nt(q_ref[lo:hi, c], k[:hi]), lo)
            o_ref[lo:hi, c] = mm(s.astype(BF16), v[:hi])


def intra(q, kv, after=()):
    tok, cols = q.shape
    return ordered(
        intra_kernel,
        after,
        (q, kv),
        in_specs=[VSPEC] * 2,
        out_specs=VSPEC,
        out_shape=jax.ShapeDtypeStruct((tok, cols), F32),
        cost_estimate=cost(4 * tok * tok * cols, 6 * tok * cols),
        name="intra",
    )


def weighted(bits_ref, refs):
    total = None
    for i, ref in enumerate(refs):
        term = ref[...].astype(F32) * bits_ref[i].astype(F32)
        total = term if total is None else total + term
    return total


def grad_kernel(n, bits_ref, q_ref, o_ref, kv_ref, gain_ref, up_ref, *refs):
    states, (dq_ref, do_ref, own_ref) = refs[:n], refs[n:]
    prev = weighted(bits_ref, states).astype(BF16)
    k, v = kv_ref[:, :HD], kv_ref[:, HD:]
    own = None
    for lo, hi in halves(q_ref.shape[0]):
        for h in range(q_ref.shape[1] // HD):
            c = slice(h * HD, (h + 1) * HD)
            q = q_ref[lo:hi, c]
            o = o_ref[lo:hi, c] + mm(q, prev)
            inv = lax.rsqrt(jnp.mean(o * o, axis=-1, keepdims=True) + EPSILON)
            scaled = gain_ref[:, c] * up_ref[lo:hi, c].astype(F32)
            along = jnp.mean(scaled * o, axis=-1, keepdims=True)
            do = (inv * (scaled - o * ((inv * inv) * along))).astype(BF16)
            do_ref[lo:hi, c] = do
            s = masked(mm_nt(do, v[:hi]), lo).astype(BF16)
            dq_ref[c, lo:hi] = (mm(s, k[:hi]) + mm_nt(do, prev)).T.astype(BF16)
            part = mm_tn(q, do)
            own = part if own is None else own + part
    own_ref[...] = own.astype(BF16)


def grad_step(bits, q, o, kv, gain, upstream, states, after=()):
    tok, cols = q.shape
    n = len(states)
    return ordered(
        functools.partial(grad_kernel, n),
        after,
        (bits, q, o, kv, gain.reshape(1, cols), upstream, *states),
        in_specs=[SSPEC] + [VSPEC] * (5 + n),
        out_specs=[VSPEC] * 3,
        out_shape=[
            jax.ShapeDtypeStruct((cols, tok), BF16),
            jax.ShapeDtypeStruct((tok, cols), BF16),
            jax.ShapeDtypeStruct((HD, HD), BF16),
        ],
        cost_estimate=cost(8 * tok * tok * cols, 12 * tok * cols),
        name="grad_step",
    )


def inner_kernel(q_ref, do_ref, kv_ref, out_ref):
    k, v = kv_ref[:, :HD], kv_ref[:, HD:]
    tok = q_ref.shape[0]
    for lo, hi in halves(tok):
        col = lax.broadcasted_iota(jnp.int32, (hi - lo, tok - lo), 1)
        row = lax.broadcasted_iota(jnp.int32, (hi - lo, tok - lo), 0)
        dk = dv = None
        for h in range(q_ref.shape[1] // HD):
            c = slice(h * HD, (h + 1) * HD)
            q, do = q_ref[lo:, c], do_ref[lo:, c]
            s = jnp.where(col >= row, mm_nt(k[lo:hi], q), 0.0).astype(BF16)
            ds = jnp.where(col >= row, mm_nt(v[lo:hi], do), 0.0).astype(BF16)
            dk_h, dv_h = mm(ds, q), mm(s, do)
            dk = dk_h if dk is None else dk + dk_h
            dv = dv_h if dv is None else dv + dv_h
        out_ref[lo:hi, :HD] = dk
        out_ref[lo:hi, HD:] = dv


def inner_step(q, do, kv, after=()):
    tok, cols = q.shape
    return ordered(
        inner_kernel,
        after,
        (q, do, kv),
        in_specs=[VSPEC] * 3,
        out_specs=VSPEC,
        out_shape=jax.ShapeDtypeStruct((tok, 2 * HD), F32),
        cost_estimate=cost(8 * tok * tok * cols, 8 * tok * cols),
        name="inner_step",
    )


def outer_kernel(n, bits_ref, inner_ref, kv_ref, dq_ref, *refs):
    states, out_ref = refs[:n], refs[n]
    later = weighted(bits_ref, states).astype(BF16)
    k, v = kv_ref[:, :HD], kv_ref[:, HD:]
    cols = dq_ref.shape[0]
    out_ref[:cols, :] = dq_ref[...]
    out_ref[cols : cols + HD, :] = (inner_ref[:, :HD] + mm_nt(v, later)).T.astype(BF16)
    out_ref[cols + HD :, :] = (inner_ref[:, HD:] + mm(k, later)).T.astype(BF16)


def outer_step(bits, inner, kv, dq, states, after=()):
    tok = kv.shape[0]
    width = dq.shape[0] + 2 * HD
    n = len(states)
    return ordered(
        functools.partial(outer_kernel, n),
        after,
        (bits, inner, kv, dq, *states),
        in_specs=[SSPEC] + [VSPEC] * (3 + n),
        out_specs=VSPEC,
        out_shape=jax.ShapeDtypeStruct((width, tok), BF16),
        cost_estimate=cost(4 * tok * HD * HD, 8 * tok * HD),
        name="outer_step",
    )


def send_kernel(ids_ref, x_ref, g_ref, out_ref):
    out_ref[0] = mm(g_ref[...], x_ref[...]).astype(BF16)


def keep_kernel(half, ids_ref, x_ref, g_ref, got_ref, high_ref, low_ref):
    total = (mm(g_ref[...], x_ref[...]) + got_ref[0].astype(F32)).astype(BF16)

    @pl.when(pl.program_id(0) < half)
    def _():
        high_ref[0] = total

    @pl.when(pl.program_id(0) >= half)
    def _():
        low_ref[0] = total


def weight_keep(x, g, got, seq, after=()):
    tok, d = x.shape
    cols = g.shape[0]
    count = lax.axis_size(seq) // 2
    half = count // 2
    blk = d // (2 * count)
    order = [(i + half) % count for i in range(count)]
    ids = jnp.stack([lax.axis_index(seq) ^ (2 * i) for i in order]).astype(jnp.int32)
    return ordered(
        functools.partial(keep_kernel, half),
        after,
        (ids, x, g, got),
        lead=1,
        grid=(count,),
        in_specs=[
            pl.BlockSpec((tok, blk), lambda i, ids: (0, ids[i])),
            pl.BlockSpec((cols, tok), lambda i, ids: (0, 0)),
            pl.BlockSpec((1, cols, blk), lambda i, ids: (lax.shift_right_logical(ids[i], 1), 0, 0)),
        ],
        out_specs=[
            pl.BlockSpec((1, cols, blk), lambda i, ids: (jnp.minimum(i, half - 1), 0, 0)),
            pl.BlockSpec((1, cols, blk), lambda i, ids: (jnp.maximum(i - half, 0), 0, 0)),
        ],
        out_shape=[jax.ShapeDtypeStruct((half, cols, blk), BF16)] * 2,
        cost_estimate=cost(2 * tok * cols * blk * count, 2 * count * blk * (tok + 2 * cols)),
        name="weight_keep",
    )


def fold_kernel(a_ref, b_ref, high_ref, low_ref):
    half = a_ref.shape[0] // 2
    total = (a_ref[...].astype(F32) + b_ref[...].astype(F32)).astype(BF16)
    low_ref[...] = total[:half]
    high_ref[...] = total[half:]


def fold(a, b):
    m, cols, blk = a.shape
    return ordered(
        fold_kernel,
        (),
        (a, b),
        in_specs=[VSPEC] * 2,
        out_specs=[VSPEC] * 2,
        out_shape=[jax.ShapeDtypeStruct((m // 2, cols, blk), BF16)] * 2,
        cost_estimate=cost(a.size, 6 * a.size),
        name="fold",
    )


def weight_send(parity, x, g, seq, after=()):
    tok, d = x.shape
    cols = g.shape[0]
    count = lax.axis_size(seq) // 2
    blk = d // (2 * count)
    return ordered(
        send_kernel,
        after,
        (parity, x, g),
        lead=1,
        grid=(count,),
        in_specs=[
            pl.BlockSpec((tok, blk), lambda i, ids: (0, 2 * i + ids[0])),
            pl.BlockSpec((cols, tok), lambda i, ids: (0, 0)),
        ],
        out_specs=pl.BlockSpec((1, cols, blk), lambda i, ids: (i, 0, 0)),
        out_shape=jax.ShapeDtypeStruct((count, cols, blk), BF16),
        cost_estimate=cost(2 * tok * cols * blk * count, 2 * count * blk * (tok + cols)),
        name="weight_send",
    )


def last_kernel(*refs):
    q_ref, kv_ref = refs[-2:]
    total = refs[0][0].astype(F32)
    for ref in refs[1:-2]:
        total = total + ref[0].astype(F32)
    blk, cols = q_ref.shape
    q_ref[...] = total[:cols].T
    kv_ref[pl.ds(0, blk, 2), :] = total[cols : cols + HD].T
    kv_ref[pl.ds(1, blk, 2), :] = total[cols + HD :].T


def weight_last(parts, after=()):
    _, width, blk = parts[0].shape
    cols = width - 2 * HD
    q, kv = ordered(
        last_kernel,
        after,
        tuple(parts),
        in_specs=[VSPEC] * len(parts),
        out_specs=[VSPEC] * 2,
        out_shape=[
            jax.ShapeDtypeStruct((blk, cols), F32),
            jax.ShapeDtypeStruct((2 * blk, HD), F32),
        ],
        cost_estimate=cost(blk * cols, 8 * blk * cols),
        name="weight_last",
    )
    return q, kv.reshape(blk, 2, HD)


def flip(array, axis, bit):
    count = lax.axis_size(axis)
    return lax.ppermute(array, axis, [(i, i ^ (1 << bit)) for i in range(count)])


def merge_kernel(a_ref, b_ref, out_ref):
    out_ref[...] = (a_ref[...].astype(F32) + b_ref[...].astype(F32)).astype(BF16)


def merge(a, b, after=()):
    return ordered(
        merge_kernel,
        after,
        (a, b),
        in_specs=[VSPEC] * 2,
        out_specs=VSPEC,
        out_shape=jax.ShapeDtypeStruct(a.shape, BF16),
        cost_estimate=cost(a.size, 6 * a.size),
        name="merge",
    )


def doubling(state, axis, levels, between):
    received = []
    done = None
    for bit in range(levels):
        got = flip(state, axis, bit)
        received.append(got)
        if bit == 0:
            done = between(got)
        if bit < levels - 1:
            state = merge(state, got, after=() if bit == 0 else (done,))
    return received, done


def partial_kernel(ids_ref, q_ref, kv_ref, g_ref, *refs):
    cols = q_ref.shape[1]
    total = mm(q_ref[...], g_ref[:cols, :]) + mm(kv_ref[...], g_ref[cols:, :])
    for ref in refs[:-1]:
        total = total + ref[...].astype(F32)
    refs[-1][...] = total.astype(BF16)


def partial(at, part, parts, ids, q_weight, wkv, grads, got, n, after=()):
    d, cols = q_weight.shape
    width, tok = grads.shape
    rows, some = d // n, tok // parts
    steps = 2
    tile = rows // steps
    out = pl.BlockSpec((tile, some), lambda i, ids: (i, 0))
    return ordered(
        partial_kernel,
        after,
        (ids, q_weight, wkv, grads, *got),
        lead=1,
        grid=(steps,),
        in_specs=[
            pl.BlockSpec((tile, cols), lambda i, ids: (ids[at] * steps + i, 0)),
            pl.BlockSpec((tile, width - cols), lambda i, ids: (ids[at] * steps + i, 0)),
            pl.BlockSpec((width, some), lambda i, ids: (0, part)),
        ]
        + [out] * len(got),
        out_specs=out,
        out_shape=jax.ShapeDtypeStruct((rows, some), BF16),
        cost_estimate=cost(2 * rows * width * some, 2 * rows * (width + 2 * some)),
        name="partial",
    )


def final_kernel(parts, *refs):
    out_ref = refs[-1]
    each = (len(refs) - 1) // parts
    some = out_ref.shape[0] // parts
    for part in range(parts):
        total = None
        for ref in refs[part * each : (part + 1) * each]:
            term = ref[...].astype(F32)
            total = term if total is None else total + term
        out_ref[part * some : (part + 1) * some, :] = total.T.astype(BF16)


def final(groups, after=()):
    arrays = [array for group in groups for array in group]
    rows, some = arrays[0].shape
    tok = some * len(groups)
    return ordered(
        functools.partial(final_kernel, len(groups)),
        after,
        tuple(arrays),
        in_specs=[VSPEC] * len(arrays),
        out_specs=VSPEC,
        out_shape=jax.ShapeDtypeStruct((tok, rows), BF16),
        cost_estimate=cost(rows * tok, 8 * rows * tok),
        name="final",
    )


LINE = ((3, 2, 1, 0, 0), (3, 3, 2, 0, 1), (0, 0, 3, 1, 2), (0, 1, 3, 2, 3))


def line_close(one, firsts, head):
    send = lambda array, pairs: lax.ppermute(array, head, pairs)
    seconds = []
    for part, first in enumerate(firsts):
        total = one(1, part, got=(first,))
        seconds.append((send(total, [(0, 1), (1, 2)]), send(total, [(3, 2), (2, 1)])))
    thirds = []
    for part, (right, left) in enumerate(seconds):
        upward = one(2, part, got=(right,))
        downward = one(3, part, got=(left,))
        thirds.append(
            [send(upward, [(0, 1), (1, 2), (2, 3)]), send(downward, [(3, 2), (2, 1), (1, 0)])]
        )
    return thirds


def body(x, q_weight, kv_weight, norm_gain, out_grad):
    seq, head = "seq", "head"
    count, n = lax.axis_size(seq), lax.axis_size(head)
    levels = (count - 1).bit_length()
    place = lax.axis_index(seq)
    bits = jnp.stack([(place >> i) & 1 for i in range(levels)]).astype(jnp.int32)
    same = (place & 1).reshape(1).astype(jnp.int32)
    kv_flat = kv_weight.reshape(2 * q_weight.shape[0], HD)

    line = jnp.array(LINE, jnp.int32)[lax.axis_index(head) % 4]
    kv, state, wkv = kv_project(x, kv_flat)
    states, q = doubling(state, seq, levels, lambda got: q_project(x, q_weight, after=(got,)))
    o = intra(q, kv, after=states[1:2])
    dq, do, own = grad_step(bits, q, o, kv, norm_gain, out_grad, states)
    laters, inner = doubling(
        own, seq, levels, lambda got: inner_step(q, do, kv, after=(got,))
    )
    grads = outer_step(1 - bits, inner, kv, dq, laters)

    filling = []
    if n == 4:
        one = functools.partial(
            partial, parts=PARTS, ids=line, q_weight=q_weight, wkv=wkv, grads=grads, n=n
        )
        filling = [one(0, part, got=()) for part in range(PARTS)]
        firsts = [lax.ppermute(array, head, [(0, 1), (3, 2)]) for array in filling]
    got = flip(weight_send(1 - same, x, grads, seq), seq, 0)
    high, low = weight_keep(x, grads, got, seq, after=filling)
    for bit in range(levels - 1, 0, -1):
        got = flip(high, seq, bit)
        if bit > 1:
            high, low = fold(low, got)
    parts = [low, got]
    q_grad, kv_grad = weight_last(parts)
    if n == 4:
        own_terms = [one(4, part, got=()) for part in range(PARTS)]
        thirds = line_close(one, firsts, head)
        groups = [[mine] + third for mine, third in zip(own_terms, thirds)]
        input_grad = final(groups, after=(q_grad,))
    else:
        both = jnp.concatenate([q_weight, wkv], axis=1)
        whole = lax.dot_general(
            grads, both, (((0,), (1,)), ((), ())), preferred_element_type=F32
        )
        input_grad = lax.psum_scatter(
            whole.astype(BF16), head, scatter_dimension=1, tiled=True
        )
    return input_grad, q_grad, kv_grad


def solution(mesh):
    return jax.shard_map(
        body,
        mesh=mesh,
        in_specs=(
            P("seq", None),
            P(None, "head"),
            P(None, None, "head"),
            P("head"),
            P("seq", "head"),
        ),
        out_specs=(P("seq", "head"), P("seq", "head"), P("seq", None, "head")),
        check_vma=False,
    )
```

```python
import functools

import jax
import jax.numpy as jnp
from jax import lax
from jax.experimental import pallas as pl
from jax.experimental.pallas import tpu as pltpu
from jax.sharding import PartitionSpec as P

HD = 128
PARTS = 2
EPSILON = 1e-05
F32 = jnp.float32
BF16 = jnp.bfloat16
VMEM_LIMIT = 18 * 1024 * 1024
VMEM_MOST = 58 * 1024 * 1024


def mm(a, b):
    return jnp.dot(a, b, preferred_element_type=F32)


def mm_nt(a, b):
    return lax.dot_general(a, b, (((1,), (1,)), ((), ())), preferred_element_type=F32)


def mm_tn(a, b):
    return lax.dot_general(a, b, (((0,), (0,)), ((), ())), preferred_element_type=F32)


def params(limit):
    return pltpu.CompilerParams(vmem_limit_bytes=limit)


def cost(flops, nbytes):
    return pl.CostEstimate(
        flops=int(flops) // 64, bytes_accessed=int(nbytes) // 64, transcendentals=0
    )


def ordered(kernel, after, args, *, in_specs, lead=0, grid=None, out_specs, scratch=(), limit=VMEM_LIMIT, **kw):
    given = len(args) - lead
    extra = len(after)

    def run(*refs):
        kernel(*refs[: lead + given], *refs[lead + given + extra :])

    in_specs = list(in_specs) + [pl.BlockSpec(memory_space=pl.ANY)] * extra
    return pl.pallas_call(
        run,
        grid_spec=pltpu.PrefetchScalarGridSpec(
            num_scalar_prefetch=lead,
            grid=grid or (),
            in_specs=in_specs,
            out_specs=out_specs,
            scratch_shapes=scratch,
        ),
        compiler_params=params(limit),
        **kw,
    )(*args, *after)


ANY = pl.BlockSpec(memory_space=pl.ANY)
VSPEC = pl.BlockSpec(memory_space=pltpu.VMEM)
SSPEC = pl.BlockSpec(memory_space=pltpu.SMEM)


def parting(rows):
    half = rows // 2
    row = lax.broadcasted_iota(jnp.int32, (rows, rows), 0)
    col = lax.broadcasted_iota(jnp.int32, (rows, rows), 1)
    target = jnp.where(row < half, 2 * row, 2 * (row - half) + 1)
    return jnp.where(col == target, 1.0, 0.0).astype(BF16)


def kv_kernel(x_ref, w_ref, kv_ref, state_ref, wkv_ref, acc_ref):
    step = pl.program_id(0)
    steps = pl.num_programs(0)
    rows = 2 * HD
    perm = parting(rows)
    for i in range(w_ref.shape[0] // rows):
        both = mm(perm, w_ref[i * rows : (i + 1) * rows, :]).astype(BF16)
        wkv_ref[i * HD : (i + 1) * HD, :HD] = both[:HD]
        wkv_ref[i * HD : (i + 1) * HD, HD:] = both[HD:]
    part = mm(x_ref[...], wkv_ref[...])

    @pl.when(step == 0)
    def _():
        acc_ref[...] = part

    @pl.when(step > 0)
    def _():
        acc_ref[...] += part

    @pl.when(step == steps - 1)
    def _():
        kv = acc_ref[...].astype(BF16)
        kv_ref[...] = kv
        state_ref[...] = mm_tn(kv[:, :HD], kv[:, HD:]).astype(BF16)


def kv_project(x, kv_flat, after=()):
    tok, d = x.shape
    steps = 4
    blk = d // steps
    return ordered(
        kv_kernel,
        after,
        (x, kv_flat),
        grid=(steps,),
        in_specs=[
            pl.BlockSpec((tok, blk), lambda i: (0, i)),
            pl.BlockSpec((2 * blk, HD), lambda i: (i, 0)),
        ],
        out_specs=[
            pl.BlockSpec((tok, 2 * HD), lambda i: (0, 0)),
            pl.BlockSpec((HD, HD), lambda i: (0, 0)),
            pl.BlockSpec((blk, 2 * HD), lambda i: (i, 0)),
        ],
        out_shape=[
            jax.ShapeDtypeStruct((tok, 2 * HD), BF16),
            jax.ShapeDtypeStruct((HD, HD), BF16),
            jax.ShapeDtypeStruct((d, 2 * HD), BF16),
        ],
        scratch=[pltpu.VMEM((tok, 2 * HD), F32)],
        cost_estimate=cost(4 * tok * d * HD, 2 * (tok * d + 4 * d * HD)),
        name="kv_project",
        limit=VMEM_MOST,
    )


def halves(tok):
    blk = min(256, tok)
    return [(lo, lo + blk) for lo in range(0, tok, blk)]


def masked(scores, row_first):
    rows, cols = scores.shape
    row = lax.broadcasted_iota(jnp.int32, (rows, cols), 0) + row_first
    col = lax.broadcasted_iota(jnp.int32, (rows, cols), 1)
    return jnp.where(col <= row, scores, 0.0)


def q_kernel(x_ref, w_ref, q_ref, acc_ref):
    step = pl.program_id(0)
    steps = pl.num_programs(0)
    part = mm(x_ref[...], w_ref[...])

    @pl.when(step == 0)
    def _():
        acc_ref[...] = part

    @pl.when((step > 0) & (step < steps - 1))
    def _():
        acc_ref[...] += part

    @pl.when(step == steps - 1)
    def _():
        q_ref[...] = (acc_ref[...] + part).astype(BF16)


def q_project(x, q_weight, after=()):
    tok, d = x.shape
    cols = q_weight.shape[1]
    steps = 4
    blk = d // steps
    return ordered(
        q_kernel,
        after,
        (x, q_weight),
        grid=(steps,),
        in_specs=[
            pl.BlockSpec((tok, blk), lambda i: (0, i)),
            pl.BlockSpec((blk, cols), lambda i: (i, 0)),
        ],
        out_specs=pl.BlockSpec((tok, cols), lambda i: (0, 0)),
        out_shape=jax.ShapeDtypeStruct((tok, cols), BF16),
        scratch=[pltpu.VMEM((tok, cols), F32)],
        cost_estimate=cost(2 * tok * d * cols, 2 * (tok * d + d * cols)),
        name="q_project",
        limit=VMEM_MOST,
    )


def intra_kernel(q_ref, kv_ref, o_ref):
    k, v = kv_ref[:, :HD], kv_ref[:, HD:]
    for lo, hi in halves(q_ref.shape[0]):
        for h in range(q_ref.shape[1] // HD):
            c = slice(h * HD, (h + 1) * HD)
            s = masked(mm_nt(q_ref[lo:hi, c], k[:hi]), lo)
            o_ref[lo:hi, c] = mm(s.astype(BF16), v[:hi])


def intra(q, kv, after=()):
    tok, cols = q.shape
    return ordered(
        intra_kernel,
        after,
        (q, kv),
        in_specs=[VSPEC] * 2,
        out_specs=VSPEC,
        out_shape=jax.ShapeDtypeStruct((tok, cols), F32),
        cost_estimate=cost(4 * tok * tok * cols, 6 * tok * cols),
        name="intra",
    )


def weighted(bits_ref, refs):
    total = None
    for i, ref in enumerate(refs):
        term = ref[...].astype(F32) * bits_ref[i].astype(F32)
        total = term if total is None else total + term
    return total


def grad_kernel(n, bits_ref, q_ref, o_ref, kv_ref, gain_ref, up_ref, *refs):
    states, (dq_ref, do_ref, own_ref) = refs[:n], refs[n:]
    prev = weighted(bits_ref, states).astype(BF16)
    k, v = kv_ref[:, :HD], kv_ref[:, HD:]
    own = None
    for lo, hi in halves(q_ref.shape[0]):
        for h in range(q_ref.shape[1] // HD):
            c = slice(h * HD, (h + 1) * HD)
            q = q_ref[lo:hi, c]
            o = o_ref[lo:hi, c] + mm(q, prev)
            inv = lax.rsqrt(jnp.mean(o * o, axis=-1, keepdims=True) + EPSILON)
            scaled = gain_ref[:, c] * up_ref[lo:hi, c].astype(F32)
            along = jnp.mean(scaled * o, axis=-1, keepdims=True)
            do = (inv * (scaled - o * ((inv * inv) * along))).astype(BF16)
            do_ref[lo:hi, c] = do
            s = masked(mm_nt(do, v[:hi]), lo).astype(BF16)
            dq_ref[c, lo:hi] = (mm(s, k[:hi]) + mm_nt(do, prev)).T.astype(BF16)
            part = mm_tn(q, do)
            own = part if own is None else own + part
    own_ref[...] = own.astype(BF16)


def grad_step(bits, q, o, kv, gain, upstream, states, after=()):
    tok, cols = q.shape
    n = len(states)
    return ordered(
        functools.partial(grad_kernel, n),
        after,
        (bits, q, o, kv, gain.reshape(1, cols), upstream, *states),
        in_specs=[SSPEC] + [VSPEC] * (5 + n),
        out_specs=[VSPEC] * 3,
        out_shape=[
            jax.ShapeDtypeStruct((cols, tok), BF16),
            jax.ShapeDtypeStruct((tok, cols), BF16),
            jax.ShapeDtypeStruct((HD, HD), BF16),
        ],
        cost_estimate=cost(8 * tok * tok * cols, 12 * tok * cols),
        name="grad_step",
    )


def inner_kernel(q_ref, do_ref, kv_ref, out_ref):
    k, v = kv_ref[:, :HD], kv_ref[:, HD:]
    tok = q_ref.shape[0]
    for lo, hi in halves(tok):
        col = lax.broadcasted_iota(jnp.int32, (hi - lo, tok - lo), 1)
        row = lax.broadcasted_iota(jnp.int32, (hi - lo, tok - lo), 0)
        dk = dv = None
        for h in range(q_ref.shape[1] // HD):
            c = slice(h * HD, (h + 1) * HD)
            q, do = q_ref[lo:, c], do_ref[lo:, c]
            s = jnp.where(col >= row, mm_nt(k[lo:hi], q), 0.0).astype(BF16)
            ds = jnp.where(col >= row, mm_nt(v[lo:hi], do), 0.0).astype(BF16)
            dk_h, dv_h = mm(ds, q), mm(s, do)
            dk = dk_h if dk is None else dk + dk_h
            dv = dv_h if dv is None else dv + dv_h
        out_ref[lo:hi, :HD] = dk
        out_ref[lo:hi, HD:] = dv


def inner_step(q, do, kv, after=()):
    tok, cols = q.shape
    return ordered(
        inner_kernel,
        after,
        (q, do, kv),
        in_specs=[VSPEC] * 3,
        out_specs=VSPEC,
        out_shape=jax.ShapeDtypeStruct((tok, 2 * HD), F32),
        cost_estimate=cost(8 * tok * tok * cols, 8 * tok * cols),
        name="inner_step",
    )


def outer_kernel(n, bits_ref, inner_ref, kv_ref, dq_ref, *refs):
    states, out_ref = refs[:n], refs[n]
    later = weighted(bits_ref, states).astype(BF16)
    k, v = kv_ref[:, :HD], kv_ref[:, HD:]
    cols = dq_ref.shape[0]
    out_ref[:cols, :] = dq_ref[...]
    out_ref[cols : cols + HD, :] = (inner_ref[:, :HD] + mm_nt(v, later)).T.astype(BF16)
    out_ref[cols + HD :, :] = (inner_ref[:, HD:] + mm(k, later)).T.astype(BF16)


def outer_step(bits, inner, kv, dq, states, after=()):
    tok = kv.shape[0]
    width = dq.shape[0] + 2 * HD
    n = len(states)
    return ordered(
        functools.partial(outer_kernel, n),
        after,
        (bits, inner, kv, dq, *states),
        in_specs=[SSPEC] + [VSPEC] * (3 + n),
        out_specs=VSPEC,
        out_shape=jax.ShapeDtypeStruct((width, tok), BF16),
        cost_estimate=cost(4 * tok * HD * HD, 8 * tok * HD),
        name="outer_step",
    )


def send_kernel(ids_ref, x_ref, g_ref, out_ref):
    out_ref[0] = mm(g_ref[...], x_ref[...]).astype(BF16)


def keep_kernel(half, ids_ref, x_ref, g_ref, got_ref, high_ref, low_ref):
    total = (mm(g_ref[...], x_ref[...]) + got_ref[0].astype(F32)).astype(BF16)

    @pl.when(pl.program_id(0) < half)
    def _():
        high_ref[0] = total

    @pl.when(pl.program_id(0) >= half)
    def _():
        low_ref[0] = total


def weight_keep(x, g, got, seq, after=()):
    tok, d = x.shape
    cols = g.shape[0]
    count = lax.axis_size(seq) // 2
    half = count // 2
    blk = d // (2 * count)
    order = [(i + half) % count for i in range(count)]
    ids = jnp.stack([lax.axis_index(seq) ^ (2 * i) for i in order]).astype(jnp.int32)
    return ordered(
        functools.partial(keep_kernel, half),
        after,
        (ids, x, g, got),
        lead=1,
        grid=(count,),
        in_specs=[
            pl.BlockSpec((tok, blk), lambda i, ids: (0, ids[i])),
            pl.BlockSpec((cols, tok), lambda i, ids: (0, 0)),
            pl.BlockSpec((1, cols, blk), lambda i, ids: (lax.shift_right_logical(ids[i], 1), 0, 0)),
        ],
        out_specs=[
            pl.BlockSpec((1, cols, blk), lambda i, ids: (jnp.minimum(i, half - 1), 0, 0)),
            pl.BlockSpec((1, cols, blk), lambda i, ids: (jnp.maximum(i - half, 0), 0, 0)),
        ],
        out_shape=[jax.ShapeDtypeStruct((half, cols, blk), BF16)] * 2,
        cost_estimate=cost(2 * tok * cols * blk * count, 2 * count * blk * (tok + 2 * cols)),
        name="weight_keep",
    )


def fold_kernel(a_ref, b_ref, high_ref, low_ref):
    half = a_ref.shape[0] // 2
    total = (a_ref[...].astype(F32) + b_ref[...].astype(F32)).astype(BF16)
    low_ref[...] = total[:half]
    high_ref[...] = total[half:]


def fold(a, b):
    m, cols, blk = a.shape
    return ordered(
        fold_kernel,
        (),
        (a, b),
        in_specs=[VSPEC] * 2,
        out_specs=[VSPEC] * 2,
        out_shape=[jax.ShapeDtypeStruct((m // 2, cols, blk), BF16)] * 2,
        cost_estimate=cost(a.size, 6 * a.size),
        name="fold",
    )


def weight_send(parity, x, g, seq, after=()):
    tok, d = x.shape
    cols = g.shape[0]
    count = lax.axis_size(seq) // 2
    blk = d // (2 * count)
    return ordered(
        send_kernel,
        after,
        (parity, x, g),
        lead=1,
        grid=(count,),
        in_specs=[
            pl.BlockSpec((tok, blk), lambda i, ids: (0, 2 * i + ids[0])),
            pl.BlockSpec((cols, tok), lambda i, ids: (0, 0)),
        ],
        out_specs=pl.BlockSpec((1, cols, blk), lambda i, ids: (i, 0, 0)),
        out_shape=jax.ShapeDtypeStruct((count, cols, blk), BF16),
        cost_estimate=cost(2 * tok * cols * blk * count, 2 * count * blk * (tok + cols)),
        name="weight_send",
        limit=VMEM_MOST,
    )


def last_kernel(*refs):
    q_ref, kv_ref = refs[-2:]
    total = refs[0][0].astype(F32)
    for ref in refs[1:-2]:
        total = total + ref[0].astype(F32)
    blk, cols = q_ref.shape
    q_ref[...] = total[:cols].T
    kv_ref[pl.ds(0, blk, 2), :] = total[cols : cols + HD].T
    kv_ref[pl.ds(1, blk, 2), :] = total[cols + HD :].T


def weight_last(parts, after=()):
    _, width, blk = parts[0].shape
    cols = width - 2 * HD
    q, kv = ordered(
        last_kernel,
        after,
        tuple(parts),
        in_specs=[VSPEC] * len(parts),
        out_specs=[VSPEC] * 2,
        out_shape=[
            jax.ShapeDtypeStruct((blk, cols), F32),
            jax.ShapeDtypeStruct((2 * blk, HD), F32),
        ],
        cost_estimate=cost(blk * cols, 8 * blk * cols),
        name="weight_last",
    )
    return q, kv.reshape(blk, 2, HD)


def flip(array, axis, bit):
    count = lax.axis_size(axis)
    return lax.ppermute(array, axis, [(i, i ^ (1 << bit)) for i in range(count)])


def merge_kernel(a_ref, b_ref, out_ref):
    out_ref[...] = (a_ref[...].astype(F32) + b_ref[...].astype(F32)).astype(BF16)


def merge(a, b, after=()):
    return ordered(
        merge_kernel,
        after,
        (a, b),
        in_specs=[VSPEC] * 2,
        out_specs=VSPEC,
        out_shape=jax.ShapeDtypeStruct(a.shape, BF16),
        cost_estimate=cost(a.size, 6 * a.size),
        name="merge",
    )


def doubling(state, axis, levels, between):
    received = []
    done = None
    for bit in range(levels):
        got = flip(state, axis, bit)
        received.append(got)
        if bit == 0:
            done = between(got)
        if bit < levels - 1:
            state = merge(state, got, after=() if bit == 0 else (done,))
    return received, done


def partial_kernel(ids_ref, q_ref, kv_ref, g_ref, *refs):
    cols = q_ref.shape[1]
    total = mm(q_ref[...], g_ref[:cols, :]) + mm(kv_ref[...], g_ref[cols:, :])
    for ref in refs[:-1]:
        total = total + ref[...].astype(F32)
    refs[-1][...] = total.astype(BF16)


def partial(at, part, parts, ids, q_weight, wkv, grads, got, n, after=()):
    d, cols = q_weight.shape
    width, tok = grads.shape
    rows, some = d // n, tok // parts
    steps = 2
    tile = rows // steps
    out = pl.BlockSpec((tile, some), lambda i, ids: (i, 0))
    return ordered(
        partial_kernel,
        after,
        (ids, q_weight, wkv, grads, *got),
        lead=1,
        grid=(steps,),
        in_specs=[
            pl.BlockSpec((tile, cols), lambda i, ids: (ids[at] * steps + i, 0)),
            pl.BlockSpec((tile, width - cols), lambda i, ids: (ids[at] * steps + i, 0)),
            pl.BlockSpec((width, some), lambda i, ids: (0, part)),
        ]
        + [out] * len(got),
        out_specs=out,
        out_shape=jax.ShapeDtypeStruct((rows, some), BF16),
        cost_estimate=cost(2 * rows * width * some, 2 * rows * (width + 2 * some)),
        name="partial",
    )


def final_kernel(parts, *refs):
    out_ref = refs[-1]
    each = (len(refs) - 1) // parts
    some = out_ref.shape[0] // parts
    for part in range(parts):
        total = None
        for ref in refs[part * each : (part + 1) * each]:
            term = ref[...].astype(F32)
            total = term if total is None else total + term
        out_ref[part * some : (part + 1) * some, :] = total.T.astype(BF16)


def final(groups, after=()):
    arrays = [array for group in groups for array in group]
    rows, some = arrays[0].shape
    tok = some * len(groups)
    return ordered(
        functools.partial(final_kernel, len(groups)),
        after,
        tuple(arrays),
        in_specs=[VSPEC] * len(arrays),
        out_specs=VSPEC,
        out_shape=jax.ShapeDtypeStruct((tok, rows), BF16),
        cost_estimate=cost(rows * tok, 8 * rows * tok),
        name="final",
    )


LINE = ((3, 2, 1, 0, 0), (3, 3, 2, 0, 1), (0, 0, 3, 1, 2), (0, 1, 3, 2, 3))


def line_close(one, firsts, head):
    send = lambda array, pairs: lax.ppermute(array, head, pairs)
    seconds = []
    for part, first in enumerate(firsts):
        total = one(1, part, got=(first,))
        seconds.append((send(total, [(0, 1), (1, 2)]), send(total, [(3, 2), (2, 1)])))
    thirds = []
    for part, (right, left) in enumerate(seconds):
        upward = one(2, part, got=(right,))
        downward = one(3, part, got=(left,))
        thirds.append(
            [send(upward, [(0, 1), (1, 2), (2, 3)]), send(downward, [(3, 2), (2, 1), (1, 0)])]
        )
    return thirds


def body(x, q_weight, kv_weight, norm_gain, out_grad):
    seq, head = "seq", "head"
    count, n = lax.axis_size(seq), lax.axis_size(head)
    levels = (count - 1).bit_length()
    place = lax.axis_index(seq)
    bits = jnp.stack([(place >> i) & 1 for i in range(levels)]).astype(jnp.int32)
    same = (place & 1).reshape(1).astype(jnp.int32)
    kv_flat = kv_weight.reshape(2 * q_weight.shape[0], HD)

    line = jnp.array(LINE, jnp.int32)[lax.axis_index(head) % 4]
    kv, state, wkv = kv_project(x, kv_flat)
    states, q = doubling(state, seq, levels, lambda got: q_project(x, q_weight, after=(got,)))
    o = intra(q, kv, after=states[1:2])
    dq, do, own = grad_step(bits, q, o, kv, norm_gain, out_grad, states)
    laters, inner = doubling(
        own, seq, levels, lambda got: inner_step(q, do, kv, after=(got,))
    )
    grads = outer_step(1 - bits, inner, kv, dq, laters)

    filling = []
    if n == 4:
        one = functools.partial(
            partial, parts=PARTS, ids=line, q_weight=q_weight, wkv=wkv, grads=grads, n=n
        )
        filling = [one(0, part, got=()) for part in range(PARTS)]
        firsts = [lax.ppermute(array, head, [(0, 1), (3, 2)]) for array in filling]
    got = flip(weight_send(1 - same, x, grads, seq), seq, 0)
    high, low = weight_keep(x, grads, got, seq, after=filling)
    for bit in range(levels - 1, 0, -1):
        got = flip(high, seq, bit)
        if bit > 1:
            high, low = fold(low, got)
    parts = [low, got]
    q_grad, kv_grad = weight_last(parts)
    if n == 4:
        own_terms = [one(4, part, got=()) for part in range(PARTS)]
        thirds = line_close(one, firsts, head)
        groups = [[mine] + third for mine, third in zip(own_terms, thirds)]
        input_grad = final(groups, after=(q_grad,))
    else:
        both = jnp.concatenate([q_weight, wkv], axis=1)
        whole = lax.dot_general(
            grads, both, (((0,), (1,)), ((), ())), preferred_element_type=F32
        )
        input_grad = lax.psum_scatter(
            whole.astype(BF16), head, scatter_dimension=1, tiled=True
        )
    return input_grad, q_grad, kv_grad


def solution(mesh):
    return jax.shard_map(
        body,
        mesh=mesh,
        in_specs=(
            P("seq", None),
            P(None, "head"),
            P(None, None, "head"),
            P("head"),
            P("seq", "head"),
        ),
        out_specs=(P("seq", "head"), P("seq", "head"), P("seq", None, "head")),
        check_vma=False,
    )
```
